32 devices in a mesh: row: 8 (over z, y), col: 4 (over x, core).
Axes of the slice: x: 2, y: 2, z: 4, core: 2. Of those that a mesh axis runs over, the one named last changes fastest.
Arguments:
- operator: bfloat16 [20480, 20480], P('row', 'col'), may hold values from -0.0625 to 0.0625
- panels: float32 [20480, 512], P(('row', 'col')), may hold values from -6 to 6
Outputs:
- adjoint: float32 [3, 20480, 512], P(None, ('row', 'col'))
The draws below stay inside these ranges and needn't reach their ends.
All inputs are finite; a program needn't handle non-finite values.
Results may differ from the reference program's by a relative error of at most 0.0043.
Values may be sent and summed in bfloat16 or wider, within the bound.
A program may use at most 128 MiB of HBM per device.

```python
import jax
import jax.numpy as jnp
from jax import lax

N = 20480
K = 512
APPS = 3


def spiked(array, key, source, target, blocks, factor):
    owner, partner = [(jnp.arange(array.shape[axis_at]) // (array.shape[axis_at] // blocks)).reshape([-1 if axis == axis_at else 1 for axis in range(array.ndim)]) for axis_at in (source, target)]
    chosen = jax.random.permutation(key, blocks)[partner]
    strong = (owner == chosen) | (owner == (partner + blocks // 2) % blocks)
    return jnp.where(strong, factor * array, array)


def shard_levels(stream_key, dims, split, low, top_value):
    gain, own = 1.0, jax.random.fold_in(stream_key, 6)
    for axis_at, parts in split:
        draws = jnp.exp(jax.random.uniform(jax.random.fold_in(own, axis_at), (parts,), jnp.float32, low / len(split), top_value / len(split)))
        gain = gain * jnp.repeat(draws, dims[axis_at] // parts).reshape([-1 if axis == axis_at else 1 for axis in range(len(dims))])
    return gain


def bell_draw(stream_key, shape, deviation, limit, shards=(), kind=jnp.bfloat16):
    result = deviation * jax.random.normal(stream_key, shape, jnp.float32)
    if shards:
        result = result * shard_levels(stream_key, shape, shards, -0.22, 0.18)
    return jnp.clip(result, -limit, limit).astype(kind)


def heavy_noise(key, shape, scale, most, shards, heavy, kind=jnp.bfloat16):
    result = scale * jax.random.normal(key, shape, jnp.float32)
    if shards:
        result = result * shard_levels(key, shape, shards, -0.22, 0.18)
    return jnp.clip(spiked(result, jax.random.fold_in(key, 3), *heavy), -most, most).astype(kind)


def setup_inputs(seed: int = 0) -> dict:
    arg_keys = jax.random.split(jax.random.key(seed), 3)
    return {
        "operator": heavy_noise(arg_keys[0], (N, N), N ** -0.5, 0.0625, ((0, 8), (1, 4)), (0, 1, 8, 2.0)),
        "panels": bell_draw(arg_keys[1], (N, K), 1.0, 6.0, ((0, 32),), jnp.float32),
    }


def reference(operator, panels):
    current = panels
    results = []
    for repeat in range(APPS):
        rounded = current.astype(jnp.bfloat16)
        current = lax.dot_general(operator, rounded, (((0,), (0,)), ((), ())), preferred_element_type=jnp.float32)
        results.append(current)
    return jnp.stack(results)
```

```python
import functools

import jax
import jax.numpy as jnp
from jax import lax
from jax.experimental import pallas as pl
from jax.experimental.pallas import tpu as pltpu
from jax.sharding import PartitionSpec as P

APPS = 3
CHUNKS = 4
LAG = 1
RELAY = 9
MESH = pl.DeviceIdType.MESH


def kernel(cols, panels_ref, op_ref, out_ref, x, own, opbuf, ysend, yrecv, fsend, bsend,
           brecv, frecv, op_sem, ys_sem, yr_sem, bs_sem, br_sem, fs_sem, fr_sem,
           xs_sem, xr_sem, x0s_sem, x0r_sem, os_sem, or_sem):
    zs = cols
    steps = CHUNKS * cols
    width = own.shape[2]
    row, col = lax.axis_index("row"), lax.axis_index("col")
    z, y = row // 2, row % 2
    root = z == col
    partner = (z * 2 + 1 - y, col)
    far = z // 2 != col // 2
    mate = jnp.logical_not(far) & (z != col)
    from_far = ((z >= col) & (z < zs - 1) & ((z + 1) // 2 != col // 2)) | (
        (z <= col) & (z > 0) & ((z - 1) // 2 != col // 2)
    )
    across = lax.rem(z + cols // 2, cols)
    relay = col == across
    sibling = col + 1 - 2 * (col % 2)
    onward = (jnp.where(z > col, row - 2, row + 2), col)
    others = [lax.rem(col + d, cols) for d in range(1, cols)]

    barrier = pltpu.get_barrier_semaphore()
    pl.semaphore_signal(barrier, inc=1, device_id=partner, device_id_type=MESH)
    for other in others:
        pl.semaphore_signal(barrier, inc=1, device_id=(row, other), device_id_type=MESH)

    @pl.when(z > 0)
    def _():
        pl.semaphore_signal(barrier, inc=1, device_id=(row - 2, col), device_id_type=MESH)

    @pl.when(z < zs - 1)
    def _():
        pl.semaphore_signal(barrier, inc=1, device_id=(row + 2, col), device_id_type=MESH)

    def op_copy(slot, step):
        half = 1 - y if slot == 0 else y
        first = pl.multiple_of((half * cols + step % cols) * width, 128)
        return pltpu.make_async_copy(
            op_ref.at[:, pl.ds(first, width)], opbuf.at[slot], op_sem.at[slot]
        )

    op_copy(0, 0).start()
    op_copy(1, 0).start()
    pl.semaphore_wait(
        barrier, cols + jnp.where(z > 0, 1, 0) + jnp.where(z < zs - 1, 1, 0)
    )

    def first_x(h, d, source):
        return pltpu.make_async_remote_copy(
            src_ref=panels_ref.at[h],
            dst_ref=x.at[0, h, source],
            send_sem=x0s_sem.at[h, d],
            recv_sem=x0r_sem.at[h, source],
            device_id=(row, others[d]),
            device_id_type=MESH,
        )

    for h in range(CHUNKS):
        for d in range(cols - 1):
            first_x(h, d, col).start()
        x[0, h, col] = panels_ref[h]

    def y_copy(app, step):
        return pltpu.make_async_remote_copy(
            src_ref=ysend.at[step],
            dst_ref=yrecv.at[app, step],
            send_sem=ys_sem.at[step],
            recv_sem=yr_sem.at[app, step],
            device_id=partner,
            device_id_type=MESH,
        )

    def bz_copy(app, step):
        return pltpu.make_async_remote_copy(
            src_ref=bsend.at[step],
            dst_ref=brecv.at[app, step],
            send_sem=bs_sem.at[step],
            recv_sem=br_sem.at[app, step],
            device_id=onward,
            device_id_type=MESH,
        )

    def fz_copy(app, step):
        return pltpu.make_async_remote_copy(
            src_ref=fsend.at[step],
            dst_ref=frecv.at[app, step],
            send_sem=fs_sem.at[step],
            recv_sem=fr_sem.at[app, step],
            device_id=onward,
            device_id_type=MESH,
        )

    def x_copy(app, step, d):
        block = x.at[app + 1, step // cols, step % cols]
        return pltpu.make_async_remote_copy(
            src_ref=block,
            dst_ref=block,
            send_sem=xs_sem.at[app, d, step],
            recv_sem=xr_sem.at[app, step],
            device_id=(row, sibling if d == 0 else across),
            device_id_type=MESH,
        )

    def out_local(app, step):
        return pltpu.make_async_copy(
            fsend.at[step], out_ref.at[app, step // cols], os_sem.at[app, step]
        )

    def out_copy(app, step):
        return pltpu.make_async_remote_copy(
            src_ref=fsend.at[step],
            dst_ref=out_ref.at[app, step // cols],
            send_sem=os_sem.at[app, step],
            recv_sem=or_sem.at[app, step // cols],
            device_id=(row, step % cols),
            device_id_type=MESH,
        )

    def out_wait(app, step):
        @pl.when(step % cols == col)
        def _():
            out_local(app, step).wait()

        @pl.when(step % cols != col)
        def _():
            out_copy(app, step).wait_send()

    def product(app, h, slot):
        total = None
        for k in range(cols):
            term = jnp.dot(
                x[app, h, k],
                opbuf[slot, k * width : (k + 1) * width, :],
                preferred_element_type=jnp.float32,
            )
            total = term if total is None else total + term
        return total

    total = APPS * steps

    def make(turn):
        app, step = turn // steps, turn % steps
        h, s = step // cols, step % cols

        @pl.when((s == 0) & (app == 0))
        def _():
            for d in range(cols - 1):
                first_x(h, d, others[d]).wait_recv()

        @pl.when((s == 0) & (app > 0) & jnp.logical_not(root) & jnp.logical_not(relay))
        def _():
            for k in range(cols):
                x_copy(app - 1, h * cols + k, 0).wait_recv()

        op_copy(0, step).wait()
        theirs = product(app, h, 0)

        @pl.when(turn < total - 1)
        def _():
            op_copy(0, step + 1).start()

        @pl.when(app > 0)
        def _():
            y_copy(app - 1, step).wait_send()

        ysend[step] = theirs.astype(jnp.bfloat16)
        y_copy(app, step).start()
        op_copy(1, step).wait()
        own[turn % (LAG + 1)] = product(app, h, 1)

        @pl.when(turn < total - 1)
        def _():
            op_copy(1, step + 1).start()

    def combine(turn):
        app, step = turn // steps, turn % steps
        h, s = step // cols, step % cols
        acc = own.at[turn % (LAG + 1)]
        y_copy(app, step).wait_recv()
        acc[...] += yrecv[app, step].astype(jnp.float32)

        @pl.when(from_far)
        def _():
            bz_copy(app, step).wait_recv()
            acc[...] += brecv[app, step].astype(jnp.float32)

        @pl.when(far)
        def _():
            @pl.when(app > 0)
            def _():
                bz_copy(app - 1, step).wait_send()

            bsend[step] = acc[...].astype(jnp.bfloat16)
            bz_copy(app, step).start()

        @pl.when(mate)
        def _():
            @pl.when(app > 0)
            def _():
                fz_copy(app - 1, step).wait_send()

            fsend[step] = acc[...]
            fz_copy(app, step).start()

        @pl.when(root)
        def _():
            fz_copy(app, step).wait_recv()
            acc[...] += frecv[app, step]

            @pl.when(app < APPS - 1)
            def _():
                x[app + 1, h, s] = acc[...].astype(jnp.bfloat16)
                x_copy(app, step, 1).start()
                x_copy(app, step, 0).start()

            @pl.when(app > 0)
            def _():
                out_wait(app - 1, step)

            fsend[step] = acc[...]

            @pl.when(s == col)
            def _():
                out_local(app, step).start()

            @pl.when(s != col)
            def _():
                out_copy(app, step).start()

    def forward(turn):
        app, step = turn // steps, turn % steps

        @pl.when(relay)
        def _():
            x_copy(app, step, 0).wait_recv()
            x_copy(app, step, 0).start()

    def one(turn, carry):
        @pl.when((turn >= LAG + RELAY) & (turn < LAG + RELAY + total - steps))
        def _():
            forward(turn - LAG - RELAY)

        @pl.when(turn < total)
        def _():
            make(turn)

        @pl.when(turn >= LAG)
        def _():
            combine(turn - LAG)

        return carry

    lax.fori_loop(0, total + LAG, one, 0)

    def finish(step, carry):
        y_copy(APPS - 1, step).wait_send()

        @pl.when(root)
        def _():
            out_wait(APPS - 1, step)
            for app in range(APPS - 1):
                x_copy(app, step, 0).wait_send()
                x_copy(app, step, 1).wait_send()

        @pl.when(relay)
        def _():
            for app in range(APPS - 1):
                x_copy(app, step, 0).wait_send()

        @pl.when(far)
        def _():
            bz_copy(APPS - 1, step).wait_send()

        @pl.when(mate)
        def _():
            fz_copy(APPS - 1, step).wait_send()

        return carry

    lax.fori_loop(0, steps, finish, 0)
    for h in range(CHUNKS):
        for d in range(cols - 1):
            first_x(h, d, col).wait_send()

    @pl.when(jnp.logical_not(root))
    def _():
        for app in range(APPS):
            for h in range(CHUNKS):
                out_copy(app, h * cols + col).wait_recv()


def by_kernel(operator, panels):
    cols = lax.axis_size("col")
    width, count = panels.shape
    part = count // CHUNKS
    steps = CHUNKS * cols
    turned = panels.astype(jnp.bfloat16).T.reshape(CHUNKS, part, width)
    block = (part, width)
    dma = pltpu.SemaphoreType.DMA
    out = pl.pallas_call(
        functools.partial(kernel, cols),
        out_shape=jax.ShapeDtypeStruct((APPS, CHUNKS) + block, jnp.float32),
        in_specs=[
            pl.BlockSpec(memory_space=pltpu.VMEM),
            pl.BlockSpec(memory_space=pl.ANY),
        ],
        out_specs=pl.BlockSpec(memory_space=pl.ANY),
        scratch_shapes=[
            pltpu.VMEM((APPS, CHUNKS, cols) + block, jnp.bfloat16),
            pltpu.VMEM((LAG + 1,) + block, jnp.float32),
            pltpu.VMEM((2, operator.shape[0], width), jnp.bfloat16),
            pltpu.VMEM((steps,) + block, jnp.bfloat16),
            pltpu.VMEM((APPS, steps) + block, jnp.bfloat16),
            pltpu.VMEM((steps,) + block, jnp.float32),
            pltpu.VMEM((steps,) + block, jnp.bfloat16),
            pltpu.VMEM((APPS, steps) + block, jnp.bfloat16),
            pltpu.VMEM((APPS, steps) + block, jnp.float32),
            dma((2,)),
            dma((steps,)),
            dma((APPS, steps)),
            dma((steps,)),
            dma((APPS, steps)),
            dma((steps,)),
            dma((APPS, steps)),
            dma((APPS - 1, 2, steps)),
            dma((APPS - 1, steps)),
            dma((CHUNKS, cols - 1)),
            dma((CHUNKS, cols)),
            dma((APPS, steps)),
            dma((APPS, CHUNKS)),
        ],
        compiler_params=pltpu.CompilerParams(
            collective_id=0, has_side_effects=True, vmem_limit_bytes=62 * 2**20
        ),
        cost_estimate=pl.CostEstimate(
            flops=APPS * 2 * operator.size * count,
            bytes_accessed=APPS * CHUNKS * operator.size * 2,
            transcendentals=0,
        ),
    )(turned, operator)
    return out.reshape(APPS, count, width).transpose(0, 2, 1)


def by_collectives(operator, panels):
    rows = lax.axis_size("row")
    cols = lax.axis_size("col")
    perm = [(r * cols + c, c * rows + r) for r in range(rows) for c in range(cols)]
    results = []
    current = panels
    for repeat in range(APPS):
        rounded = current.astype(jnp.bfloat16)
        gathered = lax.all_gather(rounded, "col", axis=0, tiled=True)
        partial = lax.dot_general(
            operator,
            gathered,
            (((0,), (0,)), ((), ())),
            preferred_element_type=jnp.float32,
        )
        mine = lax.psum_scatter(partial, "row", scatter_dimension=0, tiled=True)
        current = lax.ppermute(mine, ("row", "col"), perm)
        results.append(current)
    return jnp.stack(results)


def solution(mesh):
    fits = mesh.shape["row"] == 8 and mesh.shape["col"] == 4
    in_specs = (P("row", "col"), P(("row", "col"), None))
    out_specs = P(None, ("row", "col"), None)
    return jax.shard_map(
        by_kernel if fits else by_collectives,
        mesh=mesh,
        in_specs=in_specs,
        out_specs=out_specs,
        check_vma=False,
    )
```
